256 devices in a mesh: row: 16 (over x_hi, z), col: 16 (over x_lo, y, core).
Axes of the slice: x: 4 (x_hi: 2, x_lo: 2; x = x_hi * 2 + x_lo), y: 4, z: 8, core: 2. Of those that a mesh axis runs over, the one named last changes fastest.
Arguments:
- fine_input: bfloat16 [1, 256, 256, 320], P(None, 'row', 'col'), may hold values from -48 to 48
- fine_gain: float32 [320], replicated, may hold values from 0.1 to 1.9
- fine_shift: float32 [320], replicated, may hold values from -3 to 3
- fine_kernel: bfloat16 [3, 3, 320, 320], replicated, may hold values from -0.109375 to 0.109375
- fine_bias: float32 [320], replicated, may hold values from -3 to 3
- fine_cotangent: bfloat16 [1, 256, 256, 320], P(None, 'row', 'col'), may hold values from -6 to 6
- coarse_input: bfloat16 [1, 128, 128, 320], P(None, 'row', 'col'), may hold values from -48 to 48
- coarse_gain: float32 [320], replicated, may hold values from 0.1 to 1.9
- coarse_shift: float32 [320], replicated, may hold values from -3 to 3
- coarse_kernel: bfloat16 [3, 3, 320, 640], replicated, may hold values from -0.109375 to 0.109375
- coarse_bias: float32 [640], replicated, may hold values from -3 to 3
- coarse_cotangent: bfloat16 [1, 128, 128, 640], P(None, 'row', 'col'), may hold values from -6 to 6
Outputs:
- fine_output: bfloat16 [1, 256, 256, 320], P(None, 'row', 'col')
- fine_input_grad: bfloat16 [1, 256, 256, 320], P(None, 'row', 'col')
- fine_kernel_grad: float32 [256, 3600], P(('row', 'col'))
- fine_gain_grad: float32 [320], replicated
- fine_shift_grad: float32 [320], replicated
- fine_bias_grad: float32 [320], replicated
- coarse_output: bfloat16 [1, 128, 128, 640], P(None, 'row', 'col')
- coarse_input_grad: bfloat16 [1, 128, 128, 320], P(None, 'row', 'col')
- coarse_kernel_grad: float32 [256, 7200], P(('row', 'col'))
- coarse_gain_grad: float32 [320], replicated
- coarse_shift_grad: float32 [320], replicated
- coarse_bias_grad: float32 [640], replicated
The draws below stay inside these ranges and needn't reach their ends.
All inputs are finite; a program needn't handle non-finite values.
Results may differ from the reference program's by a relative error of at most 0.0044.
Values may be sent and summed in bfloat16 or wider, within the bound.
No kernel may reach another device: no remote copies, remote signals or barrier semaphores. Data moves between devices by JAX's collectives and lax.ppermute only.
A program may use at most 128 MiB of HBM per device.

```python
import math
import jax
import jax.numpy as jnp
from jax import lax

C0 = 320
C1 = 640
GROUPS = 32
FRAMES = 1
HEIGHT = 256
WIDTH = 256
HEIGHT1 = 128
WIDTH1 = 128
N_ROW = 16
N_COL = 16


def place_scale(row_total, col_total):
    row_pos = jnp.arange(row_total, dtype=jnp.float32) / max(row_total - 1, 1)
    col_pos = jnp.arange(col_total, dtype=jnp.float32) / max(col_total - 1, 1)
    return (0.6 + 1.2 * row_pos)[:, None] * (0.8 + 0.4 * col_pos)[None, :]


def shape_field(rough_part, key):
    key_scale, key_offset = jax.random.split(key)
    channels = rough_part.shape[3]
    channel_scale = jnp.exp(jax.random.uniform(key_scale, (channels,), jnp.float32, math.log(0.5), math.log(5.0)))
    offsets = jax.random.uniform(key_offset, (channels,), jnp.float32, -1.0, 1.0)
    spatial = place_scale(rough_part.shape[1], rough_part.shape[2])[None, :, :, None]
    field = (offsets + channel_scale * rough_part) * spatial
    return field.astype(jnp.bfloat16)


def draw_fine_input(key, part):
    key = jax.random.fold_in(key, 11)
    key_rough = jax.random.fold_in(key, 0)
    key_field = jax.random.fold_in(key, 2)
    full_shape = (FRAMES, HEIGHT, WIDTH, C0)
    rough_part = jnp.clip(jax.random.normal(key_rough, full_shape, jnp.float32), -4.0, 4.0)
    return shape_field(rough_part, key_field)


def draw_coarse_input(key, part):
    key = jax.random.fold_in(key, 23)
    key_rough = jax.random.fold_in(key, 0)
    key_field = jax.random.fold_in(key, 2)
    full_shape = (FRAMES, HEIGHT1, WIDTH1, C0)
    rough_part = jnp.clip(jax.random.normal(key_rough, full_shape, jnp.float32), -4.0, 4.0)
    return shape_field(rough_part, key_field)


def level_of(key, extent, cuts, low, largest):
    loudness, own = 1.0, jax.random.fold_in(key, 6)
    for axis_at, blocks in cuts:
        heights = jnp.exp(jax.random.uniform(jax.random.fold_in(own, axis_at), (blocks,), jnp.float32, low / len(cuts), largest / len(cuts)))
        loudness = loudness * jnp.repeat(heights, extent[axis_at] // blocks).reshape([-1 if axis == axis_at else 1 for axis in range(len(extent))])
    return loudness


def scatter_about(own_key, shape, deviation, most, cuts=(), held_as=jnp.bfloat16):
    entries = jax.random.normal(own_key, shape, jnp.float32) * deviation
    if len(cuts) > 0:
        entries = level_of(own_key, shape, cuts, -0.22, 0.18) * entries
    return jnp.clip(entries, min=-most, max=most).astype(held_as)


def setup_inputs(seed: int = 0) -> dict:
    key_of = jax.random.split(jax.random.key(seed), 13)
    fine_input = draw_fine_input(jax.random.fold_in(key_of[12], 71), 0)
    fine_gain = jnp.clip(1.0 + 0.18 * jax.random.normal(key_of[1], (C0,), jnp.float32), 0.1, 1.9)
    fine_shift = scatter_about(key_of[2], (C0,), 0.5, 3.0, (), jnp.float32)
    fine_kernel = scatter_about(key_of[3], (3, 3, C0, C0), (9 * C0) ** -0.5, 0.109375)
    fine_bias = scatter_about(key_of[4], (C0,), 0.5, 3.0, (), jnp.float32)
    fine_cotangent = scatter_about(key_of[5], (FRAMES, HEIGHT, WIDTH, C0), 1.0, 6.0, ((1, 16), (2, 16)))
    coarse_input = draw_coarse_input(jax.random.fold_in(key_of[12], 71), 0)
    coarse_gain = jnp.clip(1.0 + 0.18 * jax.random.normal(key_of[7], (C0,), jnp.float32), 0.1, 1.9)
    coarse_shift = scatter_about(key_of[8], (C0,), 0.5, 3.0, (), jnp.float32)
    coarse_kernel = scatter_about(key_of[9], (3, 3, C0, C1), (9 * C0) ** -0.5, 0.109375)
    coarse_bias = scatter_about(key_of[10], (C1,), 0.5, 3.0, (), jnp.float32)
    coarse_cotangent = scatter_about(key_of[11], (FRAMES, HEIGHT1, WIDTH1, C1), 1.0, 6.0, ((1, 16), (2, 16)))
    return {"fine_input": fine_input, "fine_gain": fine_gain, "fine_shift": fine_shift, "fine_kernel": fine_kernel, "fine_bias": fine_bias, "fine_cotangent": fine_cotangent, "coarse_input": coarse_input, "coarse_gain": coarse_gain, "coarse_shift": coarse_shift, "coarse_kernel": coarse_kernel, "coarse_bias": coarse_bias, "coarse_cotangent": coarse_cotangent}


epsilon = 1e-06

def level_frame(frame_in, gain_vec, shift_vec, kernel, bias_vec, frame_cot):
    frame_rows, frame_cols, in_chans = frame_in.shape
    out_chans = kernel.shape[3]
    size_group = in_chans // GROUPS
    values = frame_in.astype(jnp.float32).reshape(frame_rows, frame_cols, GROUPS, size_group)
    mean_value = lax.optimization_barrier(jnp.mean(values, axis=(0, 1, 3), keepdims=True))
    centred = values - mean_value
    variance = lax.optimization_barrier(jnp.mean(centred * centred, axis=(0, 1, 3), keepdims=True))
    inv_std = lax.rsqrt(variance + epsilon)
    normed = (centred * inv_std).reshape(frame_rows, frame_cols, in_chans)
    preact = normed * gain_vec + shift_vec
    hidden = jax.nn.silu(preact).astype(jnp.bfloat16)
    padded = jnp.pad(hidden, ((1, 1), (1, 1), (0, 0)))
    cot_padded = jnp.pad(frame_cot, ((1, 1), (1, 1), (0, 0)))
    cot_rows = frame_cot.reshape(-1, out_chans)
    output = jnp.zeros((frame_rows * frame_cols, out_chans), jnp.float32)
    hid_grad = jnp.zeros((frame_rows * frame_cols, in_chans), jnp.float32)
    tap_grads = []
    for row_tap in range(3):
        for col_tap in range(3):
            window = padded[row_tap:row_tap + frame_rows, col_tap:col_tap + frame_cols, :].reshape(-1, in_chans)
            output = output + jnp.dot(window, kernel[row_tap, col_tap], preferred_element_type=jnp.float32)
            tap_grads.append(jnp.dot(window.T, cot_rows, preferred_element_type=jnp.float32))
            cot_window = cot_padded[2 - row_tap:2 - row_tap + frame_rows, 2 - col_tap:2 - col_tap + frame_cols, :]
            hid_grad = hid_grad + jnp.dot(cot_window.reshape(-1, out_chans), kernel[row_tap, col_tap].T, preferred_element_type=jnp.float32)
    output = (output + bias_vec).astype(jnp.bfloat16).reshape(frame_rows, frame_cols, out_chans)
    kernel_grad = jnp.stack(tap_grads).reshape(3, 3, in_chans, out_chans)
    hid_grad = hid_grad.reshape(frame_rows, frame_cols, in_chans)
    gate_sig = jax.nn.sigmoid(preact)
    pre_grad = hid_grad * gate_sig * (1.0 + preact * (1.0 - gate_sig))
    sum_grad = lax.optimization_barrier(jnp.sum(pre_grad, axis=(0, 1)))
    sum_norm = lax.optimization_barrier(jnp.sum(pre_grad * normed, axis=(0, 1)))
    group_count = frame_rows * frame_cols * size_group
    mean_one = lax.optimization_barrier(jnp.sum((sum_grad * gain_vec).reshape(GROUPS, size_group), axis=1)) / group_count
    mean_two = lax.optimization_barrier(jnp.sum((sum_norm * gain_vec).reshape(GROUPS, size_group), axis=1)) / group_count
    scaled = (pre_grad * gain_vec).reshape(frame_rows, frame_cols, GROUPS, size_group)
    grouped_norm = normed.reshape(frame_rows, frame_cols, GROUPS, size_group)
    input_grad = inv_std * (scaled - mean_one[:, None] - grouped_norm * mean_two[:, None])
    input_grad = input_grad.reshape(frame_rows, frame_cols, in_chans).astype(jnp.bfloat16)
    bias_sum = lax.optimization_barrier(jnp.sum(cot_rows, axis=0, dtype=jnp.float32))
    return (output, input_grad, kernel_grad, sum_grad, sum_norm, bias_sum)

def level(inputs, gain_vec, shift_vec, kernel, bias_vec, cotangent):
    frames, frame_rows, frame_cols, in_chans = inputs.shape

    def one_frame(frame_pair):
        return level_frame(frame_pair[0], gain_vec, shift_vec, kernel, bias_vec, frame_pair[1])
    results = lax.map(one_frame, (inputs, cotangent))
    grad_scale = 1.0 / math.sqrt(frames * frame_rows * frame_cols)
    kernel_grad = (lax.optimization_barrier(jnp.sum(results[2], axis=0)) * grad_scale).reshape(N_ROW * N_COL, -1)
    gain_grad = lax.optimization_barrier(jnp.sum(results[4], axis=0)) * grad_scale
    shift_grad = lax.optimization_barrier(jnp.sum(results[3], axis=0)) * grad_scale
    bias_grad = lax.optimization_barrier(jnp.sum(results[5], axis=0)) * grad_scale
    return (results[0], results[1], kernel_grad, gain_grad, shift_grad, bias_grad)

def reference(fine_input, fine_gain, fine_shift, fine_kernel, fine_bias, fine_cotangent, coarse_input, coarse_gain, coarse_shift, coarse_kernel, coarse_bias, coarse_cotangent):
    fine_part = level(fine_input, fine_gain, fine_shift, fine_kernel, fine_bias, fine_cotangent)
    coarse_part = level(coarse_input, coarse_gain, coarse_shift, coarse_kernel, coarse_bias, coarse_cotangent)
    return (fine_part[0], fine_part[1], fine_part[2], fine_part[3], fine_part[4], fine_part[5], coarse_part[0], coarse_part[1], coarse_part[2], coarse_part[3], coarse_part[4], coarse_part[5])
```

```python
import math

import jax
import jax.numpy as jnp
from jax import lax
from jax.sharding import PartitionSpec as P

GROUPS = 32
epsilon = 1e-06
ROW, COL = "row", "col"
f32, bf16 = jnp.float32, jnp.bfloat16


def shift_pair(block, axis):
    to_next, to_prev = block
    count = lax.axis_size(axis)
    forward = [(i, i + 1) for i in range(count - 1)]
    backward = [(i + 1, i) for i in range(count - 1)]
    return lax.ppermute(to_next, axis, forward), lax.ppermute(to_prev, axis, backward)


def pack(parts):
    return jnp.concatenate([p.reshape(-1, 320) for p in parts], axis=0)


def unpack(packed, shapes):
    out, at = [], 0
    for shape in shapes:
        rows = math.prod(shape) // 320
        out.append(packed[at : at + rows].reshape(shape))
        at += rows
    return out


def extend_all(blocks, axis, dim):
    lows = [lax.slice_in_dim(b, 0, 1, axis=dim) for b in blocks]
    highs = [lax.slice_in_dim(b, b.shape[dim] - 1, None, axis=dim) for b in blocks]
    shapes = [p.shape for p in lows]
    from_prev, from_next = shift_pair((pack(highs), pack(lows)), axis)
    before, after = unpack(from_prev, shapes), unpack(from_next, shapes)
    return [
        jnp.concatenate([p, b, n], axis=dim) for p, b, n in zip(before, blocks, after)
    ]


def share(vector, axis):
    count = lax.axis_size(axis)
    rows = jnp.broadcast_to(vector[None, :], (count,) + vector.shape)
    return lax.all_to_all(rows, axis, 0, 0, tiled=True)


def group_sum(per_chan):
    return jnp.sum(per_chan.reshape(GROUPS, -1), axis=1)


def per_channel(stat, chans):
    return jnp.repeat(stat, chans // GROUPS)


def local_stats(block):
    chans = block.shape[-1]
    count = block.size // GROUPS
    values = block.astype(f32)
    mean = group_sum(jnp.sum(values, axis=(0, 1))) / count
    centred = values - per_channel(mean, chans)
    spread = group_sum(jnp.sum(centred * centred, axis=(0, 1)))
    return mean, spread, count


def merge_stats(stats, counts):
    scale = jnp.repeat(jnp.array(counts, f32), GROUPS)
    for axis in (COL, ROW):
        parts = share(stats, axis)
        half = parts.shape[1] // 2
        means, spreads = parts[:, :half], parts[:, half:]
        mean = jnp.mean(means, axis=0)
        spread = jnp.sum(spreads, axis=0) + scale * jnp.sum((means - mean) ** 2, axis=0)
        scale = scale * lax.axis_size(axis)
        stats = jnp.concatenate([mean, spread])
    return mean, spread / scale


def add_up(vector):
    for axis in (COL, ROW):
        vector = jnp.sum(share(vector, axis), axis=0)
    return vector


def conv(values, kernel, spec, padding):
    return lax.conv_general_dilated(
        values[None],
        kernel,
        (1, 1),
        padding,
        dimension_numbers=("NHWC", spec, "NHWC"),
        preferred_element_type=f32,
    )[0]


def activated(block, mean_c, inv_c, gain, shift):
    normed = (block.astype(f32) - mean_c) * inv_c
    preact = normed * gain + shift
    return preact * jax.nn.sigmoid(preact)


def piece_rows(count):
    return -(-2880 // count) if 2880 % count == 0 else 2880 // count + 1


def piece_start(index, count):
    return index * 2880 // count


def window_kernel(total, width):
    row_count, col_count = lax.axis_size(ROW), lax.axis_size(COL)
    col = lax.axis_index(COL)
    slot = lax.iota(jnp.int32, row_count * width)
    piece = (slot // width) * col_count + col
    wanted = piece_start(piece, total) + slot % width
    have = lax.iota(jnp.int32, 2880)
    hot = (have[:, None] == wanted[None, :]).astype(bf16)
    return hot.reshape(3, 3, 320, row_count * width)


def strip_of(gathered):
    count, rows, cols, chans = gathered.shape
    return gathered.transpose(1, 0, 2, 3).reshape(rows, count * cols, chans)


def row_valid(tile_rows):
    row = lax.axis_index(ROW)
    at = lax.iota(jnp.int32, tile_rows + 2)
    last = lax.axis_size(ROW) - 1
    return ((at > 0) | (row > 0)) & ((at < tile_rows + 1) | (row < last))


def col_valid(tile_cols):
    col = lax.axis_index(COL)
    at = lax.iota(jnp.int32, tile_cols + 2)
    last = lax.axis_size(COL) - 1
    return ((at > 0) | (col > 0)) & ((at < tile_cols + 1) | (col < last))


def per_device(*args):
    row_count, col_count = lax.axis_size(ROW), lax.axis_size(COL)
    total = row_count * col_count
    width = piece_rows(total)
    levels = (args[:6], args[6:])
    inputs = [level[0][0] for level in levels]
    cots = [level[5][0] for level in levels]

    tall = extend_all([inputs[0], cots[0], inputs[1], cots[1]], ROW, 0)
    inputs, tall = lax.optimization_barrier((inputs, tall))
    tall_x = [tall[0], tall[2]]
    gathered_c = [lax.all_gather(c, COL) for c in cots]
    gathered_x = [lax.all_gather(x, COL) for x in tall_x]
    full = extend_all(tall, COL, 1)
    full_x, full_c = [full[0], full[2]], [full[1], full[3]]

    local = [local_stats(x) for x in inputs]
    packed = jnp.concatenate([local[0][0], local[1][0], local[0][1], local[1][1]])
    mean, var = merge_stats(packed, [local[0][2], local[1][2]])
    inv = lax.rsqrt(var + epsilon)

    own = []
    vectors = []
    for index, level in enumerate(levels):
        _, gain, shift, kernel, bias, _ = level
        x, cot = inputs[index], cots[index]
        tile_rows, tile_cols, chans = x.shape
        mean_c = per_channel(mean[index * GROUPS : (index + 1) * GROUPS], chans)
        inv_c = per_channel(inv[index * GROUPS : (index + 1) * GROUPS], chans)
        hid_grad = conv(full_c[index], kernel[::-1, ::-1], "HWOI", "VALID")
        normed = (x.astype(f32) - mean_c) * inv_c
        preact = normed * gain + shift
        gate = jax.nn.sigmoid(preact)
        pre_grad = hid_grad * gate * (1.0 + preact * (1.0 - gate))
        vectors += [
            jnp.sum(pre_grad, axis=(0, 1)),
            jnp.sum(pre_grad * normed, axis=(0, 1)),
            jnp.sum(cot.astype(f32), axis=(0, 1)),
        ]
        own.append((mean_c, inv_c, normed, pre_grad))
    lengths = [v.shape[0] for v in vectors]
    sums = add_up(jnp.concatenate(vectors))
    parts, at = [], 0
    for length in lengths:
        parts.append(sums[at : at + length])
        at += length

    hot = window_kernel(total, width)
    terms = []
    outputs = []
    for index, level in enumerate(levels):
        _, gain, shift, kernel, bias, _ = level
        mean_c, inv_c = own[index][0], own[index][1]
        tile_rows, tile_cols, chans = inputs[index].shape
        scale = 1.0 / math.sqrt(tile_rows * row_count * tile_cols * col_count)
        rows_ok = row_valid(tile_rows)
        strip = activated(strip_of(gathered_x[index]), mean_c, inv_c, gain, shift)
        strip = jnp.where(rows_ok[:, None, None], strip, 0.0).astype(bf16)
        picked = conv(strip, hot, "HWIO", ((0, 0), (1, 1))).astype(bf16)
        term = lax.dot_general(
            picked.reshape(-1, picked.shape[2]),
            strip_of(gathered_c[index]).reshape(-1, kernel.shape[3]),
            (((0,), (0,)), ((), ())),
            preferred_element_type=f32,
        )
        terms.append((term * scale).astype(bf16).reshape(row_count, -1))
        hidden = activated(full_x[index], mean_c, inv_c, gain, shift)
        ok = rows_ok[:, None, None] & col_valid(tile_cols)[None, :, None]
        hidden = jnp.where(ok, hidden, 0.0).astype(bf16)
        outputs.append((conv(hidden, kernel, "HWIO", "VALID") + bias).astype(bf16)[None])
    sent = jnp.concatenate(terms, axis=1).reshape(row_count, -1, 128)
    pieces = jnp.sum(lax.all_to_all(sent, ROW, 0, 0, tiled=True).astype(f32), axis=0).reshape(-1)

    index_here = lax.axis_index(ROW) * col_count + lax.axis_index(COL)
    results, at = [], 0
    for index, level in enumerate(levels):
        _, gain, _, kernel, _, _ = level
        _, inv_c, normed, pre_grad = own[index]
        tile_rows, tile_cols, chans = inputs[index].shape
        out_chans = kernel.shape[3]
        positions = tile_rows * row_count * tile_cols * col_count
        scale = 1.0 / math.sqrt(positions)
        sum_grad, sum_norm, bias_sum = parts[3 * index : 3 * index + 3]
        per_group = positions * (chans // GROUPS)
        one = per_channel(group_sum(sum_grad * gain) / per_group, chans)
        two = per_channel(group_sum(sum_norm * gain) / per_group, chans)
        input_grad = (inv_c * (pre_grad * gain - one - normed * two)).astype(bf16)[None]
        size = 2880 * out_chans // total
        skip = index_here * size - piece_start(index_here, total) * out_chans
        held = pieces[at : at + width * out_chans]
        kernel_grad = lax.dynamic_slice_in_dim(held, skip, size)[None]
        at += width * out_chans
        results += [
            outputs[index],
            input_grad,
            kernel_grad,
            sum_norm * scale,
            sum_grad * scale,
            bias_sum * scale,
        ]
    return tuple(results)


def solution(mesh):
    tile = P(None, ROW, COL, None)
    level_in = (tile, P(), P(), P(), P(), tile)
    level_out = (tile, tile, P((ROW, COL), None), P(), P(), P())
    return jax.shard_map(
        per_device,
        mesh=mesh,
        in_specs=level_in + level_in,
        out_specs=level_out + level_out,
        check_vma=False,
    )
```

```python
import math

import jax
import jax.numpy as jnp
from jax import lax
from jax.experimental import pallas as pl
from jax.experimental.pallas import tpu as pltpu
from jax.sharding import PartitionSpec as P

GROUPS = 32
epsilon = 1e-06
ROW, COL = "row", "col"
f32, bf16 = jnp.float32, jnp.bfloat16


def shift_pair(block, axis):
    to_next, to_prev = block
    count = lax.axis_size(axis)
    forward = [(i, i + 1) for i in range(count - 1)]
    backward = [(i + 1, i) for i in range(count - 1)]
    return lax.ppermute(to_next, axis, forward), lax.ppermute(to_prev, axis, backward)


def pack(parts):
    return jnp.concatenate([p.reshape(-1, 320) for p in parts], axis=0)


def unpack(packed, shapes):
    out, at = [], 0
    for shape in shapes:
        rows = math.prod(shape) // 320
        out.append(packed[at : at + rows].reshape(shape))
        at += rows
    return out


def extend_all(blocks, axis, dim):
    lows = [lax.slice_in_dim(b, 0, 1, axis=dim) for b in blocks]
    highs = [lax.slice_in_dim(b, b.shape[dim] - 1, None, axis=dim) for b in blocks]
    shapes = [p.shape for p in lows]
    from_prev, from_next = shift_pair((pack(highs), pack(lows)), axis)
    before, after = unpack(from_prev, shapes), unpack(from_next, shapes)
    return [
        jnp.concatenate([p, b, n], axis=dim) for p, b, n in zip(before, blocks, after)
    ]


def share(vector, axis):
    count = lax.axis_size(axis)
    rows = jnp.broadcast_to(vector[None, :], (count,) + vector.shape)
    return lax.all_to_all(rows, axis, 0, 0, tiled=True)


def group_sums(per_chan):
    group = lax.iota(jnp.int32, per_chan.shape[1]) // (per_chan.shape[1] // GROUPS)
    same = (group[:, None] == group[None, :]).astype(f32)
    return jnp.dot(per_chan, same, precision=lax.Precision.HIGHEST)


def local_stats(block):
    values = block.astype(f32)
    mean = jnp.mean(values, axis=(0, 1))
    centred = values - mean
    return mean, jnp.sum(centred * centred, axis=(0, 1))


def merge_stats(stats, counts, chans):
    scale = jnp.repeat(jnp.array(counts, f32), chans)
    for axis in (COL, ROW):
        parts = share(stats, axis)
        half = parts.shape[1] // 2
        means, spreads = parts[:, :half], parts[:, half:]
        mean = jnp.mean(means, axis=0)
        spread = jnp.sum(spreads, axis=0) + scale * jnp.sum((means - mean) ** 2, axis=0)
        scale = scale * lax.axis_size(axis)
        stats = jnp.concatenate([mean, spread])
    mean, spread, scale = [v.reshape(len(counts), chans) for v in (mean, spread, scale)]
    size = chans // GROUPS
    group_mean = group_sums(mean) / size
    group_spread = group_sums(spread + scale * (mean - group_mean) ** 2)
    return group_mean, group_spread / (size * scale)


def add_up(vector):
    for axis in (COL, ROW):
        vector = jnp.sum(share(vector, axis), axis=0)
    return vector


def conv(values, kernel, spec, padding):
    return lax.conv_general_dilated(
        values[None],
        kernel,
        (1, 1),
        padding,
        dimension_numbers=("NHWC", spec, "NHWC"),
        preferred_element_type=f32,
    )[0]


def activated(block, mean_c, inv_c, gain, shift):
    normed = (block.astype(f32) - mean_c) * inv_c
    preact = normed * gain + shift
    return preact * jax.nn.sigmoid(preact)


def strip_kernel(
    fine_rows, coarse_rows, scales, last_row, info, affine, packed, out, fine_hid, coarse_hid, coarse_cot, fine_sum, coarse_sum
):
    tiles, chans = packed.shape[0], packed.shape[2]
    first = 180 * info[1]
    tap = lax.div(first, 320)
    taps = [tap, jnp.minimum(tap + 1, 8)]
    taps = [(lax.div(t, 3), lax.rem(t, 3)) for t in taps]
    fine_cols, coarse_cols = 16, 8
    fine_at = 0
    fine_cot_at = fine_at + (fine_rows + 2) * fine_cols
    coarse_at = fine_cot_at + fine_rows * fine_cols
    coarse_cot_at = coarse_at + (coarse_rows + 2) * coarse_cols
    half = coarse_rows * coarse_cols
    fine_width, coarse_width = tiles * fine_cols, tiles * coarse_cols

    def rows16(start, i):
        return packed[:, pl.ds(pl.multiple_of(start + i * 16, 16), 16), :]

    def silu(values, level):
        gain = affine[2 * level : 2 * level + 1, :].reshape(1, 1, chans)
        shift = affine[2 * level + 1 : 2 * level + 2, :].reshape(1, 1, chans)
        preact = values.astype(f32) * gain + shift
        return preact * jax.nn.sigmoid(preact)

    def two_rows(values):
        return values.reshape(tiles, 2, coarse_cols, chans)

    @pl.loop(0, fine_rows + 2)
    def _(i):
        fine_hid[i] = silu(rows16(fine_at, i), 0).reshape(fine_width, chans)

    @pl.loop(0, (coarse_rows + 2) // 2)
    def _(i):
        pair = two_rows(silu(rows16(coarse_at, i), 1))
        coarse_hid[2 * i] = pair[:, 0].reshape(coarse_width, chans)
        coarse_hid[2 * i + 1] = pair[:, 1].reshape(coarse_width, chans)

    @pl.loop(0, coarse_rows // 2)
    def _(i):
        for part in range(2):
            pair = two_rows(rows16(coarse_cot_at + part * half, i).astype(f32))
            for which in range(2):
                coarse_cot[part, 2 * i + which] = pair[:, which].reshape(coarse_width, chans).astype(bf16)

    @pl.when(info[0] == 0)
    def _():
        fine_hid[0] = jnp.zeros((fine_width, chans), f32)
        coarse_hid[0] = jnp.zeros((coarse_width, chans), f32)

    @pl.when(info[0] == last_row)
    def _():
        fine_hid[fine_rows + 1] = jnp.zeros((fine_width, chans), f32)
        coarse_hid[coarse_rows + 1] = jnp.zeros((coarse_width, chans), f32)

    fine_sum[...] = jnp.zeros_like(fine_sum)
    coarse_sum[...] = jnp.zeros_like(coarse_sum)

    def shifted(values, col_tap):
        width = values.shape[0]
        turn = jnp.where(col_tap == 0, 1, jnp.where(col_tap == 1, 0, width - 1))
        moved = pltpu.roll(values, turn, 0)
        source = lax.broadcasted_iota(jnp.int32, values.shape, 0) + col_tap
        return jnp.where((source >= 1) & (source <= width), moved, 0.0).astype(bf16)

    def outer(left, right):
        return lax.dot_general(left, right, (((0,), (0,)), ((), ())), preferred_element_type=f32)

    @pl.loop(0, fine_rows)
    def _(i):
        cot = rows16(fine_cot_at, i).reshape(fine_width, chans)
        for slot in range(2):
            hid = shifted(fine_hid[i + taps[slot][0]], taps[slot][1])
            fine_sum[slot] += outer(hid, cot)

    @pl.loop(0, coarse_rows)
    def _(i):
        for slot in range(2):
            hid = shifted(coarse_hid[i + taps[slot][0]], taps[slot][1])
            for part in range(2):
                coarse_sum[part, slot] += outer(hid, coarse_cot[part, i])

    shape = (16 * 16, 2 * chans)
    slot = lax.broadcasted_iota(jnp.int32, shape, 0)
    wanted = lax.rem(first, 320) + ((slot >> 4) * 45 >> 2) + (slot & 15)
    hot = (lax.broadcasted_iota(jnp.int32, shape, 1) == wanted).astype(f32).astype(bf16)

    def chosen(total, scale):
        rounded = (total.reshape(2 * chans, chans) * scale).astype(bf16)
        return jnp.dot(hot, rounded, preferred_element_type=f32).astype(bf16).reshape(16, 16, chans)

    out[:, 0] = chosen(fine_sum[...], scales[0])
    for part in range(2):
        out[:, 1 + part] = chosen(coarse_sum[part], scales[1])


def strip_terms(packed, affine, fine_rows, coarse_rows, scales):
    tiles, _, chans = packed.shape
    info = jnp.stack([lax.axis_index(ROW), lax.axis_index(COL)]).astype(jnp.int32)
    vmem = pl.BlockSpec(memory_space=pltpu.VMEM)
    return pl.pallas_call(
        lambda *refs: strip_kernel(fine_rows, coarse_rows, scales, lax.axis_size(ROW) - 1, *refs),
        out_shape=jax.ShapeDtypeStruct((16, 3, 16, chans), bf16),
        in_specs=[pl.BlockSpec(memory_space=pltpu.SMEM), vmem, vmem],
        out_specs=vmem,
        scratch_shapes=[
            pltpu.VMEM((fine_rows + 2, tiles * 16, chans), f32),
            pltpu.VMEM((coarse_rows + 2, tiles * 8, chans), f32),
            pltpu.VMEM((2, coarse_rows, tiles * 8, chans), bf16),
            pltpu.VMEM((2, chans, chans), f32),
            pltpu.VMEM((2, 2, chans, chans), f32),
        ],
        compiler_params=pltpu.CompilerParams(vmem_limit_bytes=40 * 2**20),
        cost_estimate=pl.CostEstimate(
            flops=3 * 2**30, bytes_accessed=10 * 2**20, transcendentals=2 * 2**20
        ),
    )(info, affine, packed)


def row_valid(tile_rows):
    row = lax.axis_index(ROW)
    at = lax.iota(jnp.int32, tile_rows + 2)
    last = lax.axis_size(ROW) - 1
    return ((at > 0) | (row > 0)) & ((at < tile_rows + 1) | (row < last))


def col_valid(tile_cols):
    col = lax.axis_index(COL)
    at = lax.iota(jnp.int32, tile_cols + 2)
    last = lax.axis_size(COL) - 1
    return ((at > 0) | (col > 0)) & ((at < tile_cols + 1) | (col < last))


def per_device(*args):
    row_count, col_count = lax.axis_size(ROW), lax.axis_size(COL)
    total = row_count * col_count
    levels = (args[:6], args[6:])
    inputs = [level[0][0] for level in levels]
    cots = [level[5][0] for level in levels]

    tall = extend_all([inputs[0], cots[0], inputs[1], cots[1]], ROW, 0)
    tall_x = [tall[0], tall[2]]
    half = cots[1].shape[2] // 2
    own_strip = pack([tall_x[0], cots[0], tall_x[1], cots[1][..., :half], cots[1][..., half:]])
    own_strip, inputs, tall = lax.optimization_barrier((own_strip, inputs, tall))
    packed_strip = lax.all_gather(own_strip, COL)

    chans = inputs[0].shape[2]
    local = [local_stats(x) for x in inputs]
    packed = jnp.concatenate([local[0][0], local[1][0], local[0][1], local[1][1]])
    packed, tall = lax.optimization_barrier((packed, tall))
    full = extend_all(tall, COL, 1)
    full_x, full_c = [full[0], full[2]], [full[1], full[3]]
    mean, var = merge_stats(packed, [x.shape[0] * x.shape[1] for x in inputs], chans)
    inv = lax.rsqrt(var + epsilon)

    own = []
    vectors = []
    for index, level in enumerate(levels):
        _, gain, shift, kernel, bias, _ = level
        x, cot = inputs[index], cots[index]
        tile_rows, tile_cols, chans = x.shape
        mean_c, inv_c = mean[index], inv[index]
        hid_grad = conv(full_c[index], kernel[::-1, ::-1], "HWOI", "VALID")
        normed = (x.astype(f32) - mean_c) * inv_c
        preact = normed * gain + shift
        gate = jax.nn.sigmoid(preact)
        pre_grad = hid_grad * gate * (1.0 + preact * (1.0 - gate))
        vectors += [
            jnp.sum(pre_grad, axis=(0, 1)),
            jnp.sum(pre_grad * normed, axis=(0, 1)),
            jnp.sum(cot.astype(f32), axis=(0, 1)),
        ]
        own.append((mean_c, inv_c, normed, pre_grad))
    lengths = [v.shape[0] for v in vectors]
    sums = add_up(jnp.concatenate(vectors))
    parts, at = [], 0
    for length in lengths:
        parts.append(sums[at : at + length])
        at += length

    affine, scales = [], []
    for index, level in enumerate(levels):
        _, gain, shift, kernel, bias, _ = level
        mean_c, inv_c = own[index][0], own[index][1]
        tile_rows, tile_cols, chans = inputs[index].shape
        scales.append(1.0 / math.sqrt(tile_rows * row_count * tile_cols * col_count))
        affine += [inv_c * gain, shift - mean_c * (inv_c * gain)]
    packed_strip, full_x = lax.optimization_barrier((packed_strip, full_x))
    terms = strip_terms(
        packed_strip, jnp.stack(affine), inputs[0].shape[0], inputs[1].shape[0], scales
    )
    arrived = lax.all_to_all(terms, ROW, 0, 0, tiled=True)
    piece = jnp.sum(arrived.astype(f32), axis=0)[:, :12]
    turned = [(i, (i % col_count) * row_count + i // col_count) for i in range(total)]
    piece = lax.ppermute(piece, (ROW, COL), turned)
    outputs = []
    for index, level in enumerate(levels):
        _, gain, shift, kernel, bias, _ = level
        mean_c, inv_c = own[index][0], own[index][1]
        tile_rows, tile_cols, chans = inputs[index].shape
        hidden = activated(full_x[index], mean_c, inv_c, gain, shift)
        ok = row_valid(tile_rows)[:, None, None] & col_valid(tile_cols)[None, :, None]
        hidden = jnp.where(ok, hidden, 0.0).astype(bf16)
        outputs.append((conv(hidden, kernel, "HWIO", "VALID") + bias).astype(bf16)[None])
    held_rows = [piece[0], jnp.concatenate([piece[1], piece[2]], axis=1)]

    results = []
    for index, level in enumerate(levels):
        _, gain, _, kernel, _, _ = level
        _, inv_c, normed, pre_grad = own[index]
        tile_rows, tile_cols, chans = inputs[index].shape
        out_chans = kernel.shape[3]
        positions = tile_rows * row_count * tile_cols * col_count
        scale = 1.0 / math.sqrt(positions)
        sum_grad, sum_norm, bias_sum = parts[3 * index : 3 * index + 3]
        per_group = positions * (chans // GROUPS)
        one, two = group_sums(jnp.stack([sum_grad * gain, sum_norm * gain])) / per_group
        input_grad = (inv_c * (pre_grad * gain - one - normed * two)).astype(bf16)[None]
        size = 2880 * out_chans // total
        skip = (lax.axis_index(COL) & 3) * (out_chans // 4)
        kernel_grad = lax.dynamic_slice_in_dim(held_rows[index].reshape(-1), skip, size)[None]
        results += [
            outputs[index],
            input_grad,
            kernel_grad,
            sum_norm * scale,
            sum_grad * scale,
            bias_sum * scale,
        ]
    return tuple(results)


def solution(mesh):
    tile = P(None, ROW, COL, None)
    level_in = (tile, P(), P(), P(), P(), tile)
    level_out = (tile, tile, P((ROW, COL), None), P(), P(), P())
    return jax.shard_map(
        per_device,
        mesh=mesh,
        in_specs=level_in + level_in,
        out_specs=level_out + level_out,
        check_vma=False,
    )
```

```python
import math

import jax
import jax.numpy as jnp
from jax import lax
from jax.experimental import pallas as pl
from jax.experimental.pallas import tpu as pltpu
from jax.sharding import PartitionSpec as P

GROUPS = 32
epsilon = 1e-06
ROW, COL = "row", "col"
f32, bf16 = jnp.float32, jnp.bfloat16


def shift_pair(block, axis):
    to_next, to_prev = block
    count = lax.axis_size(axis)
    forward = [(i, i + 1) for i in range(count - 1)]
    backward = [(i + 1, i) for i in range(count - 1)]
    return lax.ppermute(to_next, axis, forward), lax.ppermute(to_prev, axis, backward)


def pack(parts):
    return jnp.concatenate([p.reshape(-1, 320) for p in parts], axis=0)


def unpack(packed, shapes):
    out, at = [], 0
    for shape in shapes:
        rows = math.prod(shape) // 320
        out.append(packed[at : at + rows].reshape(shape))
        at += rows
    return out


def extend_all(blocks, axis, dim):
    lows = [lax.slice_in_dim(b, 0, 1, axis=dim) for b in blocks]
    highs = [lax.slice_in_dim(b, b.shape[dim] - 1, None, axis=dim) for b in blocks]
    shapes = [p.shape for p in lows]
    from_prev, from_next = shift_pair((pack(highs), pack(lows)), axis)
    before, after = unpack(from_prev, shapes), unpack(from_next, shapes)
    return [
        jnp.concatenate([p, b, n], axis=dim) for p, b, n in zip(before, blocks, after)
    ]


def share(vector, axis):
    count = lax.axis_size(axis)
    rows = jnp.broadcast_to(vector[None, :], (count,) + vector.shape)
    return lax.all_to_all(rows, axis, 0, 0, tiled=True)


def group_sums(per_chan):
    group = lax.iota(jnp.int32, per_chan.shape[1]) // (per_chan.shape[1] // GROUPS)
    same = (group[:, None] == group[None, :]).astype(f32)
    return jnp.dot(per_chan, same, precision=lax.Precision.HIGHEST)


def local_stats(block):
    values = block.astype(f32)
    mean = jnp.mean(values, axis=(0, 1))
    centred = values - mean
    return mean, jnp.sum(centred * centred, axis=(0, 1))


def merge_stats(stats, counts, chans):
    scale = jnp.repeat(jnp.array(counts, f32), chans)
    for axis in (COL, ROW):
        parts = share(stats, axis)
        half = parts.shape[1] // 2
        means, spreads = parts[:, :half], parts[:, half:]
        mean = jnp.mean(means, axis=0)
        spread = jnp.sum(spreads, axis=0) + scale * jnp.sum((means - mean) ** 2, axis=0)
        scale = scale * lax.axis_size(axis)
        stats = jnp.concatenate([mean, spread])
    mean, spread, scale = [v.reshape(len(counts), chans) for v in (mean, spread, scale)]
    size = chans // GROUPS
    group_mean = group_sums(mean) / size
    group_spread = group_sums(spread + scale * (mean - group_mean) ** 2)
    return group_mean, group_spread / (size * scale)


def add_up(vector, axis):
    return jnp.sum(share(vector, axis), axis=0)


def conv(values, kernel, spec, padding):
    return lax.conv_general_dilated(
        values[None],
        kernel,
        (1, 1),
        padding,
        dimension_numbers=("NHWC", spec, "NHWC"),
        preferred_element_type=f32,
    )[0]


def activated(block, mean_c, inv_c, gain, shift):
    normed = (block.astype(f32) - mean_c) * inv_c
    preact = normed * gain + shift
    return preact * jax.nn.sigmoid(preact)


def strip_kernel(
    fine_rows, coarse_rows, scales, last_row, info, affine, packed, out, fine_hid, coarse_hid, coarse_cot, fine_sum, coarse_sum
):
    tiles, chans = packed.shape[0], packed.shape[2]
    first = 180 * info[1]
    tap = lax.div(first, 320)
    taps = [tap, jnp.minimum(tap + 1, 8)]
    taps = [(lax.div(t, 3), lax.rem(t, 3)) for t in taps]
    fine_cols, coarse_cols = 16, 8
    fine_at = 0
    fine_cot_at = fine_at + (fine_rows + 2) * fine_cols
    coarse_at = fine_cot_at + fine_rows * fine_cols
    coarse_cot_at = coarse_at + (coarse_rows + 2) * coarse_cols
    half = coarse_rows * coarse_cols
    fine_width, coarse_width = tiles * fine_cols, tiles * coarse_cols

    def rows16(start, i):
        return packed[:, pl.ds(pl.multiple_of(start + i * 16, 16), 16), :]

    def silu(values, level):
        gain = affine[2 * level : 2 * level + 1, :].reshape(1, 1, chans)
        shift = affine[2 * level + 1 : 2 * level + 2, :].reshape(1, 1, chans)
        preact = values.astype(f32) * gain + shift
        return preact * jax.nn.sigmoid(preact)

    def two_rows(values):
        return values.reshape(tiles, 2, coarse_cols, chans)

    @pl.loop(0, fine_rows + 2)
    def _(i):
        fine_hid[i] = silu(rows16(fine_at, i), 0).reshape(fine_width, chans)

    @pl.loop(0, (coarse_rows + 2) // 2)
    def _(i):
        pair = two_rows(silu(rows16(coarse_at, i), 1))
        coarse_hid[2 * i] = pair[:, 0].reshape(coarse_width, chans)
        coarse_hid[2 * i + 1] = pair[:, 1].reshape(coarse_width, chans)

    @pl.loop(0, coarse_rows // 2)
    def _(i):
        for part in range(2):
            pair = two_rows(rows16(coarse_cot_at + part * half, i).astype(f32))
            for which in range(2):
                coarse_cot[part, 2 * i + which] = pair[:, which].reshape(coarse_width, chans).astype(bf16)

    @pl.when(info[0] == 0)
    def _():
        fine_hid[0] = jnp.zeros((fine_width, chans), f32)
        coarse_hid[0] = jnp.zeros((coarse_width, chans), f32)

    @pl.when(info[0] == last_row)
    def _():
        fine_hid[fine_rows + 1] = jnp.zeros((fine_width, chans), f32)
        coarse_hid[coarse_rows + 1] = jnp.zeros((coarse_width, chans), f32)

    fine_sum[...] = jnp.zeros_like(fine_sum)
    coarse_sum[...] = jnp.zeros_like(coarse_sum)

    def shifted(values, col_tap):
        width = values.shape[0]
        turn = jnp.where(col_tap == 0, 1, jnp.where(col_tap == 1, 0, width - 1))
        moved = pltpu.roll(values, turn, 0)
        source = lax.broadcasted_iota(jnp.int32, values.shape, 0) + col_tap
        return jnp.where((source >= 1) & (source <= width), moved, 0.0).astype(bf16)

    def add_outer(total, slot, cot_turned, hid):
        total[slot] += jnp.dot(cot_turned, hid, preferred_element_type=f32)

    @pl.loop(0, fine_rows)
    def _(i):
        cot = rows16(fine_cot_at, i).reshape(fine_width, chans).T
        for slot in range(2):
            add_outer(fine_sum, slot, cot, shifted(fine_hid[i + taps[slot][0]], taps[slot][1]))

    @pl.loop(0, coarse_rows // 2)
    def _(i):
        hids = []
        for row_tap, col_tap in taps:
            rows = [shifted(coarse_hid[2 * i + k + row_tap], col_tap) for k in range(2)]
            hids.append(jnp.concatenate(rows, axis=0))
        for part in range(2):
            cot = coarse_cot[part, pl.ds(2 * i, 2)].reshape(2 * coarse_width, chans).T
            for slot in range(2):
                add_outer(coarse_sum.at[part], slot, cot, hids[slot])

    shape = (16 * 16, chans)
    piece_row = lax.broadcasted_iota(jnp.int32, shape, 0)
    wanted = lax.rem(first, 320) + ((piece_row >> 4) * 45 >> 2) + (piece_row & 15)
    have = lax.broadcasted_iota(jnp.int32, shape, 1)
    hot = [(have + slot * chans == wanted).astype(f32).astype(bf16) for slot in range(2)]

    def chosen(total, scale):
        rows = [
            lax.dot_general(
                hot[slot],
                (total[slot] * scale).astype(bf16),
                (((1,), (1,)), ((), ())),
                preferred_element_type=f32,
            )
            for slot in range(2)
        ]
        return (rows[0] + rows[1]).astype(bf16).reshape(16, 16, chans)

    out[:, 0] = chosen(fine_sum, scales[0])
    for part in range(2):
        out[:, 1 + part] = chosen(coarse_sum.at[part], scales[1])


def strip_terms(packed, affine, fine_rows, coarse_rows, scales):
    tiles, _, chans = packed.shape
    info = jnp.stack([lax.axis_index(ROW), lax.axis_index(COL)]).astype(jnp.int32)
    vmem = pl.BlockSpec(memory_space=pltpu.VMEM)
    return pl.pallas_call(
        lambda *refs: strip_kernel(fine_rows, coarse_rows, scales, lax.axis_size(ROW) - 1, *refs),
        out_shape=jax.ShapeDtypeStruct((16, 3, 16, chans), bf16),
        in_specs=[pl.BlockSpec(memory_space=pltpu.SMEM), vmem, vmem],
        out_specs=vmem,
        scratch_shapes=[
            pltpu.VMEM((fine_rows + 2, tiles * 16, chans), f32),
            pltpu.VMEM((coarse_rows + 2, tiles * 8, chans), f32),
            pltpu.VMEM((2, coarse_rows, tiles * 8, chans), bf16),
            pltpu.VMEM((2, chans, chans), f32),
            pltpu.VMEM((2, 2, chans, chans), f32),
        ],
        compiler_params=pltpu.CompilerParams(vmem_limit_bytes=40 * 2**20),
        cost_estimate=pl.CostEstimate(
            flops=3 * 2**30, bytes_accessed=10 * 2**20, transcendentals=2 * 2**20
        ),
    )(info, affine, packed)


def row_valid(tile_rows):
    row = lax.axis_index(ROW)
    at = lax.iota(jnp.int32, tile_rows + 2)
    last = lax.axis_size(ROW) - 1
    return ((at > 0) | (row > 0)) & ((at < tile_rows + 1) | (row < last))


def col_valid(tile_cols):
    col = lax.axis_index(COL)
    at = lax.iota(jnp.int32, tile_cols + 2)
    last = lax.axis_size(COL) - 1
    return ((at > 0) | (col > 0)) & ((at < tile_cols + 1) | (col < last))


def per_device(*args):
    row_count, col_count = lax.axis_size(ROW), lax.axis_size(COL)
    total = row_count * col_count
    levels = (args[:6], args[6:])
    inputs = [level[0][0] for level in levels]
    cots = [level[5][0] for level in levels]

    tall = extend_all([inputs[0], cots[0], inputs[1], cots[1]], ROW, 0)
    tall_x = [tall[0], tall[2]]
    half, chans = cots[1].shape[2] // 2, inputs[0].shape[2]
    own_strip = pack([tall_x[0], cots[0], tall_x[1], cots[1][..., :half], cots[1][..., half:]])
    own_strip, inputs, tall = lax.optimization_barrier((own_strip, inputs, tall))
    packed_strip = lax.all_gather(own_strip.reshape(-1, 16, chans), COL, axis=0, tiled=True)
    packed_strip = packed_strip.reshape(col_count, -1, chans)

    local = [local_stats(x) for x in inputs]
    packed = jnp.concatenate([local[0][0], local[1][0], local[0][1], local[1][1]])
    packed, tall = lax.optimization_barrier((packed, tall))
    full = extend_all(tall, COL, 1)
    full_x, full_c = [full[0], full[2]], [full[1], full[3]]
    mean, var = merge_stats(packed, [x.shape[0] * x.shape[1] for x in inputs], chans)
    inv = lax.rsqrt(var + epsilon)

    own = []
    vectors = []
    for index, level in enumerate(levels):
        _, gain, shift, kernel, bias, _ = level
        x, cot = inputs[index], cots[index]
        tile_rows, tile_cols, chans = x.shape
        mean_c, inv_c = mean[index], inv[index]
        hid_grad = conv(full_c[index], kernel[::-1, ::-1], "HWOI", "VALID")
        normed = (x.astype(f32) - mean_c) * inv_c
        preact = normed * gain + shift
        gate = jax.nn.sigmoid(preact)
        pre_grad = hid_grad * gate * (1.0 + preact * (1.0 - gate))
        vectors += [
            jnp.sum(pre_grad, axis=(0, 1)),
            jnp.sum(pre_grad * normed, axis=(0, 1)),
            jnp.sum(cot.astype(f32), axis=(0, 1)),
        ]
        own.append((mean_c, inv_c, normed, pre_grad))
    lengths = [v.shape[0] for v in vectors]
    sums = add_up(jnp.concatenate(vectors), COL)

    affine, scales = [], []
    for index, level in enumerate(levels):
        _, gain, shift, kernel, bias, _ = level
        mean_c, inv_c = own[index][0], own[index][1]
        tile_rows, tile_cols, chans = inputs[index].shape
        scales.append(1.0 / math.sqrt(tile_rows * row_count * tile_cols * col_count))
        affine += [inv_c * gain, shift - mean_c * (inv_c * gain)]
    terms = strip_terms(
        packed_strip, jnp.stack(affine), inputs[0].shape[0], inputs[1].shape[0], scales
    )
    terms, sums = lax.optimization_barrier((terms, sums))
    arrived = lax.all_to_all(terms, ROW, 0, 0, tiled=True)
    sums = add_up(sums, ROW)
    parts, at = [], 0
    for length in lengths:
        parts.append(sums[at : at + length])
        at += length
    piece = jnp.sum(arrived.astype(f32), axis=0)[:, :12]
    turned = [(i, (i % col_count) * row_count + i // col_count) for i in range(total)]
    piece = lax.ppermute(piece, (ROW, COL), turned)
    outputs = []
    for index, level in enumerate(levels):
        _, gain, shift, kernel, bias, _ = level
        mean_c, inv_c = own[index][0], own[index][1]
        tile_rows, tile_cols, chans = inputs[index].shape
        hidden = activated(full_x[index], mean_c, inv_c, gain, shift)
        ok = row_valid(tile_rows)[:, None, None] & col_valid(tile_cols)[None, :, None]
        hidden = jnp.where(ok, hidden, 0.0).astype(bf16)
        outputs.append((conv(hidden, kernel, "HWIO", "VALID") + bias).astype(bf16)[None])
    held_rows = [piece[0], jnp.concatenate([piece[1], piece[2]], axis=1)]

    results = []
    for index, level in enumerate(levels):
        _, gain, _, kernel, _, _ = level
        _, inv_c, normed, pre_grad = own[index]
        tile_rows, tile_cols, chans = inputs[index].shape
        out_chans = kernel.shape[3]
        positions = tile_rows * row_count * tile_cols * col_count
        scale = 1.0 / math.sqrt(positions)
        sum_grad, sum_norm, bias_sum = parts[3 * index : 3 * index + 3]
        per_group = positions * (chans // GROUPS)
        one, two = group_sums(jnp.stack([sum_grad * gain, sum_norm * gain])) / per_group
        input_grad = (inv_c * (pre_grad * gain - one - normed * two)).astype(bf16)[None]
        size = 2880 * out_chans // total
        skip = (lax.axis_index(COL) & 3) * (out_chans // 4)
        kernel_grad = lax.dynamic_slice_in_dim(held_rows[index].reshape(-1), skip, size)[None]
        results += [
            outputs[index],
            input_grad,
            kernel_grad,
            sum_norm * scale,
            sum_grad * scale,
            bias_sum * scale,
        ]
    return tuple(results)


def solution(mesh):
    tile = P(None, ROW, COL, None)
    level_in = (tile, P(), P(), P(), P(), tile)
    level_out = (tile, tile, P((ROW, COL), None), P(), P(), P())
    return jax.shard_map(
        per_device,
        mesh=mesh,
        in_specs=level_in + level_in,
        out_specs=level_out + level_out,
        check_vma=False,
    )
```

```python
import math

import jax
import jax.numpy as jnp
from jax import lax
from jax.experimental import pallas as pl
from jax.experimental.pallas import tpu as pltpu
from jax.sharding import PartitionSpec as P

GROUPS = 32
epsilon = 1e-06
ROW, COL = "row", "col"
f32, bf16 = jnp.float32, jnp.bfloat16


def shift_pair(block, axis):
    to_next, to_prev = block
    count = lax.axis_size(axis)
    forward = [(i, i + 1) for i in range(count - 1)]
    backward = [(i + 1, i) for i in range(count - 1)]
    return lax.ppermute(to_next, axis, forward), lax.ppermute(to_prev, axis, backward)


def pack(parts):
    return jnp.concatenate([p.reshape(-1, 320) for p in parts], axis=0)


def unpack(packed, shapes):
    out, at = [], 0
    for shape in shapes:
        rows = math.prod(shape) // 320
        out.append(packed[at : at + rows].reshape(shape))
        at += rows
    return out


def extend_all(blocks, axis, dim):
    lows = [lax.slice_in_dim(b, 0, 1, axis=dim) for b in blocks]
    highs = [lax.slice_in_dim(b, b.shape[dim] - 1, None, axis=dim) for b in blocks]
    shapes = [p.shape for p in lows]
    from_prev, from_next = shift_pair((pack(highs), pack(lows)), axis)
    before, after = unpack(from_prev, shapes), unpack(from_next, shapes)
    return [
        jnp.concatenate([p, b, n], axis=dim) for p, b, n in zip(before, blocks, after)
    ]


def share(vector, axis):
    count = lax.axis_size(axis)
    rows = jnp.broadcast_to(vector[None, :], (count,) + vector.shape)
    return lax.all_to_all(rows, axis, 0, 0, tiled=True)


def group_sums(per_chan):
    group = lax.iota(jnp.int32, per_chan.shape[1]) // (per_chan.shape[1] // GROUPS)
    same = (group[:, None] == group[None, :]).astype(f32)
    return jnp.dot(per_chan, same, precision=lax.Precision.HIGHEST)


def local_stats(block):
    values = block.astype(f32)
    mean = jnp.mean(values, axis=(0, 1))
    centred = values - mean
    return mean, jnp.sum(centred * centred, axis=(0, 1))


def merge_stats(stats, counts, chans):
    scale = jnp.repeat(jnp.array(counts, f32), chans)
    for axis in (COL, ROW):
        parts = share(stats, axis)
        half = parts.shape[1] // 2
        means, spreads = parts[:, :half], parts[:, half:]
        mean = jnp.mean(means, axis=0)
        spread = jnp.sum(spreads, axis=0) + scale * jnp.sum((means - mean) ** 2, axis=0)
        scale = scale * lax.axis_size(axis)
        stats = jnp.concatenate([mean, spread])
    mean, spread, scale = [v.reshape(len(counts), chans) for v in (mean, spread, scale)]
    size = chans // GROUPS
    group_mean = group_sums(mean) / size
    group_spread = group_sums(spread + scale * (mean - group_mean) ** 2)
    return group_mean, group_spread / (size * scale)


def add_up(vector, axis):
    return jnp.sum(share(vector, axis), axis=0)


def conv(values, kernel, spec, padding):
    return lax.conv_general_dilated(
        values[None],
        kernel,
        (1, 1),
        padding,
        dimension_numbers=("NHWC", spec, "NHWC"),
        preferred_element_type=f32,
    )[0]


def activated(block, mean_c, inv_c, gain, shift):
    normed = (block.astype(f32) - mean_c) * inv_c
    preact = normed * gain + shift
    return preact * jax.nn.sigmoid(preact)


def strip_kernel(
    fine_rows, coarse_rows, scales, last_row, info, affine, extra, packed, out, fine_hid, coarse_hid, coarse_cot, fine_sum, coarse_sum
):
    tiles, chans = packed.shape[0], packed.shape[2]
    first = 180 * info[1]
    tap = lax.div(first, 320)
    taps = [tap, jnp.minimum(tap + 1, 8)]
    taps = [(lax.div(t, 3), lax.rem(t, 3)) for t in taps]
    fine_cols, coarse_cols = 16, 8
    fine_at = 0
    fine_cot_at = fine_at + (fine_rows + 2) * fine_cols
    coarse_at = fine_cot_at + fine_rows * fine_cols
    coarse_cot_at = coarse_at + (coarse_rows + 2) * coarse_cols
    half = coarse_rows * coarse_cols
    fine_width, coarse_width = tiles * fine_cols, tiles * coarse_cols

    def rows16(start, i):
        return packed[:, pl.ds(pl.multiple_of(start + i * 16, 16), 16), :]

    def silu(values, level):
        gain = affine[2 * level : 2 * level + 1, :].reshape(1, 1, chans)
        shift = affine[2 * level + 1 : 2 * level + 2, :].reshape(1, 1, chans)
        preact = values.astype(f32) * gain + shift
        return preact * jax.nn.sigmoid(preact)

    def two_rows(values):
        return values.reshape(tiles, 2, coarse_cols, chans)

    @pl.loop(0, fine_rows + 2)
    def _(i):
        fine_hid[i] = silu(rows16(fine_at, i), 0).reshape(fine_width, chans)

    @pl.loop(0, (coarse_rows + 2) // 2)
    def _(i):
        pair = two_rows(silu(rows16(coarse_at, i), 1))
        coarse_hid[2 * i] = pair[:, 0].reshape(coarse_width, chans)
        coarse_hid[2 * i + 1] = pair[:, 1].reshape(coarse_width, chans)

    @pl.loop(0, coarse_rows // 2)
    def _(i):
        for part in range(2):
            pair = two_rows(rows16(coarse_cot_at + part * half, i).astype(f32))
            for which in range(2):
                coarse_cot[part, 2 * i + which] = pair[:, which].reshape(coarse_width, chans).astype(bf16)

    @pl.when(info[0] == 0)
    def _():
        fine_hid[0] = jnp.zeros((fine_width, chans), f32)
        coarse_hid[0] = jnp.zeros((coarse_width, chans), f32)

    @pl.when(info[0] == last_row)
    def _():
        fine_hid[fine_rows + 1] = jnp.zeros((fine_width, chans), f32)
        coarse_hid[coarse_rows + 1] = jnp.zeros((coarse_width, chans), f32)

    fine_sum[...] = jnp.zeros_like(fine_sum)
    coarse_sum[...] = jnp.zeros_like(coarse_sum)

    def shifted(values, col_tap):
        width = values.shape[0]
        turn = jnp.where(col_tap == 0, 1, jnp.where(col_tap == 1, 0, width - 1))
        moved = pltpu.roll(values, turn, 0)
        source = lax.broadcasted_iota(jnp.int32, values.shape, 0) + col_tap
        return jnp.where((source >= 1) & (source <= width), moved, 0.0).astype(bf16)

    def add_outer(total, slot, cot_turned, hid):
        total[slot] += jnp.dot(cot_turned, hid, preferred_element_type=f32)

    @pl.loop(0, fine_rows)
    def _(i):
        cot = rows16(fine_cot_at, i).reshape(fine_width, chans).T
        for slot in range(2):
            add_outer(fine_sum, slot, cot, shifted(fine_hid[i + taps[slot][0]], taps[slot][1]))

    @pl.loop(0, coarse_rows // 2)
    def _(i):
        hids = []
        for row_tap, col_tap in taps:
            rows = [shifted(coarse_hid[2 * i + k + row_tap], col_tap) for k in range(2)]
            hids.append(jnp.concatenate(rows, axis=0))
        for part in range(2):
            cot = coarse_cot[part, pl.ds(2 * i, 2)].reshape(2 * coarse_width, chans).T
            for slot in range(2):
                add_outer(coarse_sum.at[part], slot, cot, hids[slot])

    shape = (16 * 16, chans)
    piece_row = lax.broadcasted_iota(jnp.int32, shape, 0)
    wanted = lax.rem(first, 320) + ((piece_row >> 4) * 45 >> 2) + (piece_row & 15)
    have = lax.broadcasted_iota(jnp.int32, shape, 1)
    hot = [(have + slot * chans == wanted).astype(f32).astype(bf16) for slot in range(2)]

    def chosen(total, scale):
        rows = [
            lax.dot_general(
                hot[slot],
                (total[slot] * scale).astype(bf16),
                (((1,), (1,)), ((), ())),
                preferred_element_type=f32,
            )
            for slot in range(2)
        ]
        return (rows[0] + rows[1]).astype(bf16).reshape(16, 16, chans)

    out[:, 0] = chosen(fine_sum, scales[0])
    for part in range(2):
        out[:, 1 + part] = chosen(coarse_sum.at[part], scales[1])
    out[:, 3] = jnp.broadcast_to(extra[...][None], (16, 16, chans))


def strip_terms(packed, affine, extra, fine_rows, coarse_rows, scales):
    tiles, _, chans = packed.shape
    info = jnp.stack([lax.axis_index(ROW), lax.axis_index(COL)]).astype(jnp.int32)
    vmem = pl.BlockSpec(memory_space=pltpu.VMEM)
    return pl.pallas_call(
        lambda *refs: strip_kernel(fine_rows, coarse_rows, scales, lax.axis_size(ROW) - 1, *refs),
        out_shape=jax.ShapeDtypeStruct((16, 4, 16, chans), bf16),
        in_specs=[pl.BlockSpec(memory_space=pltpu.SMEM), vmem, vmem, vmem],
        out_specs=vmem,
        scratch_shapes=[
            pltpu.VMEM((fine_rows + 2, tiles * 16, chans), f32),
            pltpu.VMEM((coarse_rows + 2, tiles * 8, chans), f32),
            pltpu.VMEM((2, coarse_rows, tiles * 8, chans), bf16),
            pltpu.VMEM((2, chans, chans), f32),
            pltpu.VMEM((2, 2, chans, chans), f32),
        ],
        compiler_params=pltpu.CompilerParams(vmem_limit_bytes=40 * 2**20),
        cost_estimate=pl.CostEstimate(
            flops=3 * 2**30, bytes_accessed=10 * 2**20, transcendentals=2 * 2**20
        ),
    )(info, affine, extra, packed)


def row_valid(tile_rows):
    row = lax.axis_index(ROW)
    at = lax.iota(jnp.int32, tile_rows + 2)
    last = lax.axis_size(ROW) - 1
    return ((at > 0) | (row > 0)) & ((at < tile_rows + 1) | (row < last))


def col_valid(tile_cols):
    col = lax.axis_index(COL)
    at = lax.iota(jnp.int32, tile_cols + 2)
    last = lax.axis_size(COL) - 1
    return ((at > 0) | (col > 0)) & ((at < tile_cols + 1) | (col < last))


def per_device(*args):
    row_count, col_count = lax.axis_size(ROW), lax.axis_size(COL)
    total = row_count * col_count
    levels = (args[:6], args[6:])
    inputs = [level[0][0] for level in levels]
    cots = [level[5][0] for level in levels]

    tall = extend_all([inputs[0], cots[0], inputs[1], cots[1]], ROW, 0)
    tall_x = [tall[0], tall[2]]
    half, chans = cots[1].shape[2] // 2, inputs[0].shape[2]
    own_strip = pack([tall_x[0], cots[0], tall_x[1], cots[1][..., :half], cots[1][..., half:]])
    own_strip, inputs, tall = lax.optimization_barrier((own_strip, inputs, tall))
    packed_strip = lax.all_gather(own_strip.reshape(-1, 16, chans), COL, axis=0, tiled=True)
    packed_strip = packed_strip.reshape(col_count, -1, chans)

    local = [local_stats(x) for x in inputs]
    packed = jnp.concatenate([local[0][0], local[1][0], local[0][1], local[1][1]])
    packed, tall = lax.optimization_barrier((packed, tall))
    full = extend_all(tall, COL, 1)
    full_x, full_c = [full[0], full[2]], [full[1], full[3]]
    mean, var = merge_stats(packed, [x.shape[0] * x.shape[1] for x in inputs], chans)
    inv = lax.rsqrt(var + epsilon)

    own = []
    vectors = []
    for index, level in enumerate(levels):
        _, gain, shift, kernel, bias, _ = level
        x, cot = inputs[index], cots[index]
        tile_rows, tile_cols, chans = x.shape
        mean_c, inv_c = mean[index], inv[index]
        hid_grad = conv(full_c[index], kernel[::-1, ::-1], "HWOI", "VALID")
        normed = (x.astype(f32) - mean_c) * inv_c
        preact = normed * gain + shift
        gate = jax.nn.sigmoid(preact)
        pre_grad = hid_grad * gate * (1.0 + preact * (1.0 - gate))
        vectors += [
            jnp.sum(pre_grad, axis=(0, 1)),
            jnp.sum(pre_grad * normed, axis=(0, 1)),
            jnp.sum(cot.astype(f32), axis=(0, 1)),
        ]
        own.append((mean_c, inv_c, normed, pre_grad))
    lengths = [v.shape[0] for v in vectors]
    sums = add_up(jnp.concatenate(vectors), COL)

    affine, scales = [], []
    for index, level in enumerate(levels):
        _, gain, shift, kernel, bias, _ = level
        mean_c, inv_c = own[index][0], own[index][1]
        tile_rows, tile_cols, chans = inputs[index].shape
        scales.append(1.0 / math.sqrt(tile_rows * row_count * tile_cols * col_count))
        affine += [inv_c * gain, shift - mean_c * (inv_c * gain)]
    values = sums.reshape(-1, chans)
    coarse_part = lax.reduce_precision(values, 8, 7)
    fine_part = lax.reduce_precision(values - coarse_part, 8, 7)
    spare = jnp.zeros((16 - 2 * values.shape[0], chans), f32)
    extra = jnp.concatenate([coarse_part, fine_part, spare]).astype(bf16)
    terms = strip_terms(
        packed_strip, jnp.stack(affine), extra, inputs[0].shape[0], inputs[1].shape[0], scales
    )
    terms, full_x[1] = lax.optimization_barrier((terms, full_x[1]))
    arrived = jnp.sum(lax.all_to_all(terms, ROW, 0, 0, tiled=True).astype(f32), axis=0)
    piece = arrived[:3, :12]
    sums = (arrived[3, : values.shape[0]] + arrived[3, values.shape[0] : 2 * values.shape[0]]).reshape(-1)
    parts, at = [], 0
    for length in lengths:
        parts.append(sums[at : at + length])
        at += length
    turned = [(i, (i % col_count) * row_count + i // col_count) for i in range(total)]
    piece = lax.ppermute(piece, (ROW, COL), turned)
    outputs = []
    for index, level in enumerate(levels):
        _, gain, shift, kernel, bias, _ = level
        mean_c, inv_c = own[index][0], own[index][1]
        tile_rows, tile_cols, chans = inputs[index].shape
        hidden = activated(full_x[index], mean_c, inv_c, gain, shift)
        ok = row_valid(tile_rows)[:, None, None] & col_valid(tile_cols)[None, :, None]
        hidden = jnp.where(ok, hidden, 0.0).astype(bf16)
        outputs.append((conv(hidden, kernel, "HWIO", "VALID") + bias).astype(bf16)[None])
    held_rows = [piece[0], jnp.concatenate([piece[1], piece[2]], axis=1)]

    results = []
    for index, level in enumerate(levels):
        _, gain, _, kernel, _, _ = level
        _, inv_c, normed, pre_grad = own[index]
        tile_rows, tile_cols, chans = inputs[index].shape
        out_chans = kernel.shape[3]
        positions = tile_rows * row_count * tile_cols * col_count
        scale = 1.0 / math.sqrt(positions)
        sum_grad, sum_norm, bias_sum = parts[3 * index : 3 * index + 3]
        per_group = positions * (chans // GROUPS)
        one, two = group_sums(jnp.stack([sum_grad * gain, sum_norm * gain])) / per_group
        input_grad = (inv_c * (pre_grad * gain - one - normed * two)).astype(bf16)[None]
        size = 2880 * out_chans // total
        skip = (lax.axis_index(COL) & 3) * (out_chans // 4)
        kernel_grad = lax.dynamic_slice_in_dim(held_rows[index].reshape(-1), skip, size)[None]
        results += [
            outputs[index],
            input_grad,
            kernel_grad,
            sum_norm * scale,
            sum_grad * scale,
            bias_sum * scale,
        ]
    return tuple(results)


def solution(mesh):
    tile = P(None, ROW, COL, None)
    level_in = (tile, P(), P(), P(), P(), tile)
    level_out = (tile, tile, P((ROW, COL), None), P(), P(), P())
    return jax.shard_map(
        per_device,
        mesh=mesh,
        in_specs=level_in + level_in,
        out_specs=level_out + level_out,
        check_vma=False,
    )
```

```python
import math

import jax
import jax.numpy as jnp
from jax import lax
from jax.experimental import pallas as pl
from jax.experimental.pallas import tpu as pltpu
from jax.sharding import PartitionSpec as P

GROUPS = 32
epsilon = 1e-06
ROW, COL = "row", "col"
f32, bf16 = jnp.float32, jnp.bfloat16


def shift_pair(block, axis):
    to_next, to_prev = block
    count = lax.axis_size(axis)
    forward = [(i, i + 1) for i in range(count - 1)]
    backward = [(i + 1, i) for i in range(count - 1)]
    return lax.ppermute(to_next, axis, forward), lax.ppermute(to_prev, axis, backward)


def pack(parts):
    return jnp.concatenate([p.reshape(-1, 320) for p in parts], axis=0)


def unpack(packed, shapes):
    out, at = [], 0
    for shape in shapes:
        rows = math.prod(shape) // 320
        out.append(packed[at : at + rows].reshape(shape))
        at += rows
    return out


def extend_all(blocks, axis, dim):
    lows = [lax.slice_in_dim(b, 0, 1, axis=dim) for b in blocks]
    highs = [lax.slice_in_dim(b, b.shape[dim] - 1, None, axis=dim) for b in blocks]
    shapes = [p.shape for p in lows]
    from_prev, from_next = shift_pair((pack(highs), pack(lows)), axis)
    before, after = unpack(from_prev, shapes), unpack(from_next, shapes)
    return [
        jnp.concatenate([p, b, n], axis=dim) for p, b, n in zip(before, blocks, after)
    ]


def share(vector, axis):
    count = lax.axis_size(axis)
    rows = jnp.broadcast_to(vector[None, :], (count,) + vector.shape)
    return lax.all_to_all(rows, axis, 0, 0, tiled=True)


def group_sums(per_chan):
    group = lax.iota(jnp.int32, per_chan.shape[1]) // (per_chan.shape[1] // GROUPS)
    same = (group[:, None] == group[None, :]).astype(f32)
    return jnp.dot(per_chan, same, precision=lax.Precision.HIGHEST)


def local_stats(block):
    values = block.astype(f32)
    mean = jnp.mean(values, axis=(0, 1))
    centred = values - mean
    return mean, jnp.sum(centred * centred, axis=(0, 1))


def merge_stage(stats, sums, scale, axis):
    parts = share(jnp.concatenate([stats, sums]), axis)
    half = stats.shape[0] // 2
    means, spreads = parts[:, :half], parts[:, half : 2 * half]
    mean = jnp.mean(means, axis=0)
    spread = jnp.sum(spreads, axis=0) + scale * jnp.sum((means - mean) ** 2, axis=0)
    return jnp.concatenate([mean, spread]), jnp.sum(parts[:, 2 * half :], axis=0)


def group_stats(stats, scale, chans):
    mean, spread = stats.reshape(2, -1, chans)
    scale = scale.reshape(-1, chans)
    size = chans // GROUPS
    group_mean = group_sums(mean) / size
    group_spread = group_sums(spread + scale * (mean - group_mean) ** 2)
    return group_mean, group_spread / (size * scale)


def add_up(vector, axis):
    return jnp.sum(share(vector, axis), axis=0)


def conv(values, kernel, spec, padding):
    return lax.conv_general_dilated(
        values[None],
        kernel,
        (1, 1),
        padding,
        dimension_numbers=("NHWC", spec, "NHWC"),
        preferred_element_type=f32,
    )[0]


def activated(block, mean_c, inv_c, gain, shift):
    normed = (block.astype(f32) - mean_c) * inv_c
    preact = normed * gain + shift
    return preact * jax.nn.sigmoid(preact)


def strip_kernel(
    fine_rows, coarse_rows, scales, last_row, info, affine, extra, packed, out, fine_hid, coarse_hid, coarse_cot, fine_sum, coarse_sum
):
    tiles, chans = packed.shape[0], packed.shape[2]
    first = 180 * info[1]
    tap = lax.div(first, 320)
    taps = [tap, jnp.minimum(tap + 1, 8)]
    taps = [(lax.div(t, 3), lax.rem(t, 3)) for t in taps]
    fine_cols, coarse_cols = 16, 8
    fine_at = 0
    fine_cot_at = fine_at + (fine_rows + 2) * fine_cols
    coarse_at = fine_cot_at + fine_rows * fine_cols
    coarse_cot_at = coarse_at + (coarse_rows + 2) * coarse_cols
    half = coarse_rows * coarse_cols
    fine_width, coarse_width = tiles * fine_cols, tiles * coarse_cols

    def rows16(start, i):
        return packed[:, pl.ds(pl.multiple_of(start + i * 16, 16), 16), :]

    def silu(values, level):
        gain = affine[2 * level : 2 * level + 1, :].reshape(1, 1, chans)
        shift = affine[2 * level + 1 : 2 * level + 2, :].reshape(1, 1, chans)
        preact = values.astype(f32) * gain + shift
        return preact * jax.nn.sigmoid(preact)

    def two_rows(values):
        return values.reshape(tiles, 2, coarse_cols, chans)

    @pl.loop(0, fine_rows + 2)
    def _(i):
        fine_hid[i] = silu(rows16(fine_at, i), 0).reshape(fine_width, chans)

    @pl.loop(0, (coarse_rows + 2) // 2)
    def _(i):
        pair = two_rows(silu(rows16(coarse_at, i), 1))
        coarse_hid[2 * i] = pair[:, 0].reshape(coarse_width, chans)
        coarse_hid[2 * i + 1] = pair[:, 1].reshape(coarse_width, chans)

    @pl.loop(0, coarse_rows // 2)
    def _(i):
        for part in range(2):
            pair = two_rows(rows16(coarse_cot_at + part * half, i).astype(f32))
            for which in range(2):
                coarse_cot[part, 2 * i + which] = pair[:, which].reshape(coarse_width, chans).astype(bf16)

    @pl.when(info[0] == 0)
    def _():
        fine_hid[0] = jnp.zeros((fine_width, chans), f32)
        coarse_hid[0] = jnp.zeros((coarse_width, chans), f32)

    @pl.when(info[0] == last_row)
    def _():
        fine_hid[fine_rows + 1] = jnp.zeros((fine_width, chans), f32)
        coarse_hid[coarse_rows + 1] = jnp.zeros((coarse_width, chans), f32)

    fine_sum[...] = jnp.zeros_like(fine_sum)
    coarse_sum[...] = jnp.zeros_like(coarse_sum)

    def shifted(values, col_tap):
        width = values.shape[0]
        turn = jnp.where(col_tap == 0, 1, jnp.where(col_tap == 1, 0, width - 1))
        moved = pltpu.roll(values, turn, 0)
        source = lax.broadcasted_iota(jnp.int32, values.shape, 0) + col_tap
        return jnp.where((source >= 1) & (source <= width), moved, 0.0).astype(bf16)

    def add_outer(total, slot, cot_turned, hid):
        total[slot] += jnp.dot(cot_turned, hid, preferred_element_type=f32)

    @pl.loop(0, fine_rows)
    def _(i):
        cot = rows16(fine_cot_at, i).reshape(fine_width, chans).T
        for slot in range(2):
            add_outer(fine_sum, slot, cot, shifted(fine_hid[i + taps[slot][0]], taps[slot][1]))

    @pl.loop(0, coarse_rows // 2)
    def _(i):
        hids = []
        for row_tap, col_tap in taps:
            rows = [shifted(coarse_hid[2 * i + k + row_tap], col_tap) for k in range(2)]
            hids.append(jnp.concatenate(rows, axis=0))
        for part in range(2):
            cot = coarse_cot[part, pl.ds(2 * i, 2)].reshape(2 * coarse_width, chans).T
            for slot in range(2):
                add_outer(coarse_sum.at[part], slot, cot, hids[slot])

    shape = (16 * 16, chans)
    piece_row = lax.broadcasted_iota(jnp.int32, shape, 0)
    at = piece_row & 15
    wanted = lax.rem(first, 320) + ((piece_row >> 4) * 45 >> 2) + at
    wanted = jnp.where(at < 12, wanted, -1)
    have = lax.broadcasted_iota(jnp.int32, shape, 1)
    hot = [(have + slot * chans == wanted).astype(f32).astype(bf16) for slot in range(2)]

    spare_at = lax.broadcasted_iota(jnp.int32, (16 * 16, 16), 0) & 15
    spare_have = lax.broadcasted_iota(jnp.int32, (16 * 16, 16), 1)

    def chosen(total, scale, block):
        spare = ((spare_at >= 12) & (spare_have == 4 * block + spare_at - 12)).astype(f32).astype(bf16)
        rows = [
            lax.dot_general(
                hot[slot],
                (total[slot] * scale).astype(bf16),
                (((1,), (1,)), ((), ())),
                preferred_element_type=f32,
            )
            for slot in range(2)
        ]
        rows.append(jnp.dot(spare, extra[...], preferred_element_type=f32))
        return (rows[0] + rows[1] + rows[2]).astype(bf16).reshape(16, 16, chans)

    out[:, 0] = chosen(fine_sum, scales[0], 0)
    for part in range(2):
        out[:, 1 + part] = chosen(coarse_sum.at[part], scales[1], 1 + part)


def strip_terms(packed, affine, extra, fine_rows, coarse_rows, scales):
    tiles, _, chans = packed.shape
    info = jnp.stack([lax.axis_index(ROW), lax.axis_index(COL)]).astype(jnp.int32)
    vmem = pl.BlockSpec(memory_space=pltpu.VMEM)
    return pl.pallas_call(
        lambda *refs: strip_kernel(fine_rows, coarse_rows, scales, lax.axis_size(ROW) - 1, *refs),
        out_shape=jax.ShapeDtypeStruct((16, 3, 16, chans), bf16),
        in_specs=[pl.BlockSpec(memory_space=pltpu.SMEM), vmem, vmem, vmem],
        out_specs=vmem,
        scratch_shapes=[
            pltpu.VMEM((fine_rows + 2, tiles * 16, chans), f32),
            pltpu.VMEM((coarse_rows + 2, tiles * 8, chans), f32),
            pltpu.VMEM((2, coarse_rows, tiles * 8, chans), bf16),
            pltpu.VMEM((2, chans, chans), f32),
            pltpu.VMEM((2, 2, chans, chans), f32),
        ],
        compiler_params=pltpu.CompilerParams(vmem_limit_bytes=40 * 2**20),
        cost_estimate=pl.CostEstimate(
            flops=3 * 2**30, bytes_accessed=10 * 2**20, transcendentals=2 * 2**20
        ),
    )(info, affine, extra, packed)


def row_valid(tile_rows):
    row = lax.axis_index(ROW)
    at = lax.iota(jnp.int32, tile_rows + 2)
    last = lax.axis_size(ROW) - 1
    return ((at > 0) | (row > 0)) & ((at < tile_rows + 1) | (row < last))


def col_valid(tile_cols):
    col = lax.axis_index(COL)
    at = lax.iota(jnp.int32, tile_cols + 2)
    last = lax.axis_size(COL) - 1
    return ((at > 0) | (col > 0)) & ((at < tile_cols + 1) | (col < last))


def per_device(*args):
    row_count, col_count = lax.axis_size(ROW), lax.axis_size(COL)
    total = row_count * col_count
    levels = (args[:6], args[6:])
    inputs = [level[0][0] for level in levels]
    cots = [level[5][0] for level in levels]

    tall = extend_all([inputs[0], cots[0], inputs[1], cots[1]], ROW, 0)
    tall_x = [tall[0], tall[2]]
    half, chans = cots[1].shape[2] // 2, inputs[0].shape[2]
    own_strip = pack([tall_x[0], cots[0], tall_x[1], cots[1][..., :half], cots[1][..., half:]])
    own_strip, inputs, tall = lax.optimization_barrier((own_strip, inputs, tall))
    packed_strip = lax.all_gather(own_strip.reshape(-1, 16, chans), COL, axis=0, tiled=True)
    packed_strip = packed_strip.reshape(col_count, -1, chans)

    local = [local_stats(x) for x in inputs]
    stats = jnp.concatenate([local[0][0], local[1][0], local[0][1], local[1][1]])
    bias_sums = jnp.concatenate([jnp.sum(c.astype(f32), axis=(0, 1)) for c in cots])
    counts = [x.shape[0] * x.shape[1] for x in inputs]
    counts = jnp.repeat(jnp.array(counts, f32), chans)
    stats, bias_sums, tall = lax.optimization_barrier((stats, bias_sums, tall))
    full = extend_all(tall, COL, 1)
    stats, bias_sums = merge_stage(stats, bias_sums, counts, COL)
    full, stats = lax.optimization_barrier((full, stats))
    full_x, full_c = [full[0], full[2]], [full[1], full[3]]
    counts = counts * col_count
    stats, bias_sums = merge_stage(stats, bias_sums, counts, ROW)
    mean, var = group_stats(stats, counts * row_count, chans)
    inv = lax.rsqrt(var + epsilon)

    own = []
    vectors = []
    for index, level in enumerate(levels):
        _, gain, shift, kernel, bias, _ = level
        x = inputs[index]
        tile_rows, tile_cols, chans = x.shape
        mean_c, inv_c = mean[index], inv[index]
        hid_grad = conv(full_c[index], kernel[::-1, ::-1], "HWOI", "VALID")
        normed = (x.astype(f32) - mean_c) * inv_c
        preact = normed * gain + shift
        gate = jax.nn.sigmoid(preact)
        pre_grad = hid_grad * gate * (1.0 + preact * (1.0 - gate))
        vectors += [
            jnp.sum(pre_grad, axis=(0, 1)),
            jnp.sum(pre_grad * normed, axis=(0, 1)),
        ]
        own.append((mean_c, inv_c, normed, pre_grad))
    lengths = [v.shape[0] for v in vectors]
    sums = add_up(jnp.concatenate(vectors), COL)

    affine, scales = [], []
    for index, level in enumerate(levels):
        _, gain, shift, kernel, bias, _ = level
        mean_c, inv_c = own[index][0], own[index][1]
        tile_rows, tile_cols, chans = inputs[index].shape
        scales.append(1.0 / math.sqrt(tile_rows * row_count * tile_cols * col_count))
        affine += [inv_c * gain, shift - mean_c * (inv_c * gain)]
    values = sums.reshape(-1, chans)
    coarse_part = lax.reduce_precision(values, 8, 7)
    fine_part = lax.reduce_precision(values - coarse_part, 8, 7)
    spare = jnp.zeros((16 - 2 * values.shape[0], chans), f32)
    extra = jnp.concatenate([coarse_part, fine_part, spare]).astype(bf16)
    terms = strip_terms(
        packed_strip, jnp.stack(affine), extra, inputs[0].shape[0], inputs[1].shape[0], scales
    )
    terms, full_x = lax.optimization_barrier((terms, full_x))
    arrived = jnp.sum(lax.all_to_all(terms, ROW, 0, 0, tiled=True).astype(f32), axis=0)
    piece, spare = arrived[:, :12], arrived[:, 12:].reshape(-1, chans)
    sums = (spare[: values.shape[0]] + spare[values.shape[0] : 2 * values.shape[0]]).reshape(-1)
    parts, at = [], 0
    for length in lengths:
        parts.append(sums[at : at + length])
        at += length
    turned = [(i, (i % col_count) * row_count + i // col_count) for i in range(total)]
    piece = lax.ppermute(piece, (ROW, COL), turned)
    outputs = []
    for index, level in enumerate(levels):
        _, gain, shift, kernel, bias, _ = level
        mean_c, inv_c = own[index][0], own[index][1]
        tile_rows, tile_cols, chans = inputs[index].shape
        hidden = activated(full_x[index], mean_c, inv_c, gain, shift)
        ok = row_valid(tile_rows)[:, None, None] & col_valid(tile_cols)[None, :, None]
        hidden = jnp.where(ok, hidden, 0.0).astype(bf16)
        outputs.append((conv(hidden, kernel, "HWIO", "VALID") + bias).astype(bf16)[None])
    held_rows = [piece[0], jnp.concatenate([piece[1], piece[2]], axis=1)]

    results = []
    for index, level in enumerate(levels):
        _, gain, _, kernel, _, _ = level
        _, inv_c, normed, pre_grad = own[index]
        tile_rows, tile_cols, chans = inputs[index].shape
        out_chans = kernel.shape[3]
        positions = tile_rows * row_count * tile_cols * col_count
        scale = 1.0 / math.sqrt(positions)
        sum_grad, sum_norm = parts[2 * index : 2 * index + 2]
        bias_sum = bias_sums[:chans] if index == 0 else bias_sums[chans:]
        per_group = positions * (chans // GROUPS)
        one, two = group_sums(jnp.stack([sum_grad * gain, sum_norm * gain])) / per_group
        input_grad = (inv_c * (pre_grad * gain - one - normed * two)).astype(bf16)[None]
        size = 2880 * out_chans // total
        skip = (lax.axis_index(COL) & 3) * (out_chans // 4)
        kernel_grad = lax.dynamic_slice_in_dim(held_rows[index].reshape(-1), skip, size)[None]
        results += [
            outputs[index],
            input_grad,
            kernel_grad,
            sum_norm * scale,
            sum_grad * scale,
            bias_sum * scale,
        ]
    return tuple(results)


def solution(mesh):
    tile = P(None, ROW, COL, None)
    level_in = (tile, P(), P(), P(), P(), tile)
    level_out = (tile, tile, P((ROW, COL), None), P(), P(), P())
    return jax.shard_map(
        per_device,
        mesh=mesh,
        in_specs=level_in + level_in,
        out_specs=level_out + level_out,
        check_vma=False,
    )
```
